32 devices in a mesh: groups: 2 (over x), wide: 16 (over z, y, core).
Axes of the slice: x: 2, y: 2, z: 4, core: 2. Of those that a mesh axis runs over, the one named last changes fastest.
Arguments:
- features: bfloat16 [4096, 512], P(('groups', 'wide')), parts along dimension 0, may hold values from -3.5 to 3.5
- centres: bfloat16 [8192, 512], P(('groups', 'wide')), parts along dimension 0, may hold values from -3.5 to 3.5
- targets: bfloat16 [4096, 128], P(('groups', 'wide')), parts along dimension 0, may hold values from -8 to 8
- coefficients: float32 [8192, 128], P(('groups', 'wide')), parts along dimension 0, may hold values from -1.6 to 1.6
- momentum: float32 [8192, 128], P(('groups', 'wide')), parts along dimension 0, may hold values from -0.8 to 0.8
- block_inverse: float32 [32, 256, 256], P(('groups', 'wide')), parts along dimension 0, may hold values from -3 to 3
Outputs:
- residual: float32 [4096, 128], P(('groups', 'wide')), parts along dimension 0
- new_momentum: float32 [8192, 128], P(('groups', 'wide')), parts along dimension 0
- new_coefficients: float32 [8192, 128], P(('groups', 'wide')), parts along dimension 0
The draws below stay inside these ranges and needn't reach their ends.
There are 2 independent parts, one for each index of `groups`. The reference program is written for one: setup_inputs(seed, part) draws one part's arguments, and reference() takes and returns one part's arrays. A program takes and returns all parts, laid end to end along the dimension named above; each array names one. Nothing has to cross between parts.
All inputs are finite; a program needn't handle non-finite values.
Results may differ from the reference program's by a relative error of at most 0.0033.
Values may be sent and summed in bfloat16 or wider, within the bound.
A program may use at most 128 MiB of HBM per device.

```python
import jax
import jax.numpy as jnp
from jax import lax

D = 512
OUTS = 128
BLOCK = 256
BATCH = 2048
CENTRES = 4096


def cluster_layout(key):
    clusters = max(CENTRES // 64, 4)
    supers = max(clusters // 32, 2)
    parent = jax.random.randint(jax.random.fold_in(key, 103), (clusters,), 0, supers)
    coarse = jax.random.normal(jax.random.fold_in(key, 101), (supers, D), jnp.float32) * 0.7071
    offset = jax.random.normal(jax.random.fold_in(key, 102), (clusters, D), jnp.float32) * 0.7071
    return (coarse[parent] + offset, clusters)


def draw_points(key, stream, row_count):
    cluster_mean, clusters = cluster_layout(key)
    member = jax.random.randint(jax.random.fold_in(key, stream), (row_count,), 0, clusters)
    jitter = jax.random.normal(jax.random.fold_in(key, stream + 1), (row_count, D), jnp.float32) * 0.4
    return jnp.clip(cluster_mean[member] + jitter, -3.5, 3.5).astype(jnp.bfloat16)


def draw_features(key, part):
    return draw_points(key, 1, BATCH)


def draw_centres(key, part):
    return draw_points(key, 3, CENTRES)


def with_spikes(result, key, source, target, shards_of, factor):
    owner, partner = [(jnp.arange(result.shape[axis_at]) // (result.shape[axis_at] // shards_of)).reshape([-1 if axis == axis_at else 1 for axis in range(result.ndim)]) for axis_at in (source, target)]
    chosen = jax.random.permutation(key, shards_of)[partner]
    strong = (owner == chosen) | (owner == (partner + shards_of // 2) % shards_of)
    return jnp.where(strong, factor * result, result)


def block_levels(key, extent, shards, low, high):
    def one(axis_at, parts):
        steps = jax.random.uniform(jax.random.fold_in(jax.random.fold_in(key, 6), axis_at), (parts,), jnp.float32, low / len(shards), high / len(shards))
        return jnp.repeat(jnp.exp(steps), extent[axis_at] // parts).reshape((-1,) + (1,) * (len(extent) - axis_at - 1))

    level = one(*shards[0])
    for cut in shards[1:]:
        level = level * one(*cut)
    return level


def normal_values(stream_key, dims, width, reach, cuts=(), dtype=jnp.bfloat16):
    array = jax.random.normal(stream_key, dims, jnp.float32) * width
    if len(cuts) > 0:
        array = block_levels(stream_key, dims, cuts, -0.22, 0.18) * array
    return jnp.clip(array, min=-reach, max=reach).astype(dtype)


def bell_draw_with(own_key, extent, width, reach, cuts, heavy, kind=jnp.bfloat16):
    drawn = width * jax.random.normal(own_key, extent, jnp.float32)
    if cuts:
        drawn = drawn * block_levels(own_key, extent, cuts, -0.22, 0.18)
    return jnp.clip(with_spikes(drawn, jax.random.fold_in(own_key, 3), *heavy), -reach, reach).astype(kind)


def setup_inputs(seed: int = 0, part: int = 0) -> dict:
    key_of = jax.random.split(jax.random.key(seed), 7)
    own_keys = jax.random.split(jax.random.fold_in(key_of[6], part), 7)
    return {
        "features": draw_features(jax.random.fold_in(jax.random.fold_in(key_of[6], part), 71), part),
        "centres": draw_centres(jax.random.fold_in(jax.random.fold_in(key_of[6], part), 71), part),
        "targets": bell_draw_with(own_keys[2], (BATCH, OUTS), 1.0, 8.0, ((0, 16),), (0, 1, 16, 2.0)),
        "coefficients": bell_draw_with(own_keys[3], (CENTRES, OUTS), 0.2, 1.6, ((0, 16),), (0, 1, 16, 2.0), jnp.float32),
        "momentum": normal_values(own_keys[4], (CENTRES, OUTS), 0.1, 0.8, ((0, 16),), jnp.float32),
        "block_inverse": normal_values(own_keys[5], (CENTRES // BLOCK, BLOCK, BLOCK), 4 ** -0.5, 3.0, ((0, 16),), jnp.float32),
    }


def kernel_tile(shard_rows, row_norms, centre_block):
    centre_norms = jnp.sum(centre_block.astype(jnp.float32) ** 2, axis=1)
    products = jnp.dot(shard_rows, centre_block.T, preferred_element_type=jnp.float32)
    return jnp.exp((2.0 * products - row_norms[:, None] - centre_norms[None, :]) * (2.0 / D)).astype(jnp.bfloat16)


def reference(features, centres, targets, coefficients, momentum, block_inverse):
    row_norms = jnp.sum(features.astype(jnp.float32) ** 2, axis=1)
    nblocks = CENTRES // BLOCK
    centre_blocks = centres.reshape(nblocks, BLOCK, D)
    coef_blocks = coefficients.astype(jnp.bfloat16).reshape(nblocks, BLOCK, OUTS)

    def accumulate(running, block_pair):
        centre_block, coef_block = block_pair
        kernel = kernel_tile(features, row_norms, centre_block)
        return running + jnp.dot(kernel, coef_block, preferred_element_type=jnp.float32), None

    prediction, _ = lax.scan(accumulate, jnp.zeros((BATCH, OUTS), jnp.float32), (centre_blocks, coef_blocks))
    residual = prediction - targets.astype(jnp.float32)
    residual_half = residual.astype(jnp.bfloat16)

    def gradient_block(centre_block):
        kernel = kernel_tile(features, row_norms, centre_block)
        return lax.dot_general(kernel, residual_half, (((0,), (0,)), ((), ())), preferred_element_type=jnp.float32)

    gradient = lax.map(gradient_block, centre_blocks)
    conditioned = jnp.einsum("bij,bjk->bik", block_inverse, gradient, precision=lax.Precision.HIGHEST)
    new_momentum = 0.9 * momentum + conditioned.reshape(CENTRES, OUTS) / BATCH
    new_coefficients = coefficients - 0.5 * new_momentum
    return residual, new_momentum, new_coefficients
```

```python
import functools

import jax
import jax.numpy as jnp
from jax import lax
from jax.experimental import pallas as pl
from jax.experimental.pallas import tpu as pltpu
from jax.sharding import PartitionSpec as P

MESH = pl.DeviceIdType.MESH
PRED = jnp.float32
GRAD = jnp.float32


def kernel(
    A, B, batch,
    feat, cen, targ, coef, mom, inv,
    res_out, mom_out, coef_out,
    rows, rnorm, cens, cnorm, coefs, kt, own_pred, pred_tx, pred_rx, resid, g_own, g_tx, g_rx,
    row_ss, row_rs, cen_ss, cen_rs, cf_ss, cf_rs, pr_ss, pr_rs, re_ss, re_rs, g_ss, g_rs,
):
    w = lax.axis_index("wide")
    c = lax.rem(w, 2)
    chip = w // 2
    b = lax.rem(chip, B)
    a = chip // B
    R = feat.shape[0]
    scale = 2.0 / feat.shape[1]

    def dev(aa, bb, cc):
        return {"wide": (aa * B + bb) * 2 + cc}

    def put(src, dst, ss, rs, to):
        return pltpu.make_async_remote_copy(
            src_ref=src, dst_ref=dst, send_sem=ss, recv_sem=rs, device_id=to, device_id_type=MESH
        )

    me_cb = b * 2 + c
    mate_cb = b * 2 + (1 - c)
    mate = dev(a, b, 1 - c)

    barrier = pltpu.get_barrier_semaphore()
    for j in range(1, A):
        pl.semaphore_signal(barrier, inc=1, device_id=dev(lax.rem(a + j, A), b, c), device_id_type=MESH)
    for j in range(B):
        for k in range(2):
            if j or k:
                pl.semaphore_signal(
                    barrier, inc=1, device_id=dev(a, lax.rem(b + j, B), lax.rem(c + k, 2)), device_id_type=MESH
                )

    rows[a] = feat[...]
    cens[me_cb] = cen[...]
    coefs[me_cb] = coef[...].astype(jnp.bfloat16).T

    def row_copy(block, d):
        to = a + 1 if d == 0 else a - 1
        return put(rows.at[block], rows.at[block], row_ss.at[block, d], row_rs.at[block], dev(to, b, c))

    def cen_copy(cb, slot, to):
        return put(cens.at[cb], cens.at[cb], cen_ss.at[slot], cen_rs.at[cb], to)

    def coef_copy(cb, slot, to):
        return put(coefs.at[cb], coefs.at[cb], cf_ss.at[slot], cf_rs.at[cb], to)

    pl.semaphore_wait(barrier, A - 1 + 2 * B - 1)

    @pl.when(a < A - 1)
    def _():
        row_copy(a, 0).start()

    @pl.when(a > 0)
    def _():
        row_copy(a, 1).start()

    for j in range(1, B):
        bb = lax.rem(b + j, B)
        cen_copy(me_cb, bb, dev(a, bb, c)).start()
        coef_copy(me_cb, bb, dev(a, bb, c)).start()
    cen_copy(me_cb, B + b, mate).start()
    coef_copy(me_cb, B + b, mate).start()

    def row_norm(block):
        x = rows[block].astype(jnp.float32)
        s = jnp.sum(x * x, axis=1, keepdims=True)
        rnorm[block] = jnp.broadcast_to(s, (R, 128)).T[0:8]

    def cen_norm(cb):
        x = cens[cb].astype(jnp.float32)
        s = jnp.sum(x * x, axis=1, keepdims=True)
        cnorm[cb] = jnp.broadcast_to(s, (x.shape[0], 128))

    def tile(block, cb):
        p = lax.dot_general(
            cens[cb], rows[block], (((1,), (1,)), ((), ())), preferred_element_type=jnp.float32
        )
        e = (2.0 * p - rnorm[block, 0:1, :] - cnorm[cb, :, 0:1]) * scale
        kt[cb, :, pl.ds(pl.multiple_of(block * R, R), R)] = jnp.exp(e).astype(jnp.bfloat16)

    def tiles(block, lo, hi):
        def step(i, carry):
            tile(block, lax.rem(b + i // 2, B) * 2 + lax.rem(c + lax.rem(i, 2), 2))
            return carry

        lax.fori_loop(lo, hi, step, 0, unroll=2)

    def predict(block):
        def step(i, acc):
            k = kt[i, :, pl.ds(pl.multiple_of(block * R, R), R)]
            return acc + jnp.dot(coefs[i], k, preferred_element_type=jnp.float32)

        return lax.fori_loop(0, 2 * B, step, jnp.zeros((coefs.shape[1], R), jnp.float32), unroll=2)

    def pred_copy(block):
        return put(pred_tx.at[block], pred_rx.at[a], pr_ss.at[block], pr_rs.at[a], dev(block, b, c))

    def predict_and_send(block):
        pred_tx[block] = predict(block).astype(PRED)
        pred_copy(block).start()

    def each_at(dist, fn):
        @pl.when(a - dist >= 0)
        def _():
            fn(a - dist, 0)

        @pl.when(a + dist < A)
        def _():
            fn(a + dist, 1)

    def take_rows(block, d):
        row_copy(block, d).wait_recv()
        if d == 0:
            @pl.when(a < A - 1)
            def _():
                row_copy(block, 0).start()
        else:
            @pl.when(a > 0)
            def _():
                row_copy(block, 1).start()
        row_norm(block)
        tiles(block, 0, 2)

    row_norm(a)
    cen_norm(me_cb)
    tile(a, me_cb)
    cen_copy(mate_cb, 0, mate).wait_recv()
    coef_copy(mate_cb, 0, mate).wait_recv()
    cen_norm(mate_cb)
    tile(a, mate_cb)

    each_at(1, take_rows)

    for j in range(1, B):
        bb = lax.rem(b + j, B)
        cen_copy(bb * 2 + c, 0, mate).wait_recv()
        cen_copy(bb * 2 + c, B + bb, mate).start()
        coef_copy(bb * 2 + c, 0, mate).wait_recv()
        coef_copy(bb * 2 + c, B + bb, mate).start()
        cen_norm(bb * 2 + c)

    for dist in range(2, A - 1):
        each_at(dist, take_rows)

    for j in range(1, B):
        bb = lax.rem(b + j, B)
        cen_copy(bb * 2 + 1 - c, 0, mate).wait_recv()
        coef_copy(bb * 2 + 1 - c, 0, mate).wait_recv()
        cen_norm(bb * 2 + 1 - c)

    def finish(block, d):
        tiles(block, 2, 2 * B)
        predict_and_send(block)

    for dist in range(1, A - 1):
        each_at(dist, finish)
    tiles(a, 2, 2 * B)
    own_pred[...] = predict(a)

    def last(block, d):
        take_rows(block, d)
        finish(block, d)

    each_at(A - 1, last)

    total = own_pred[...]
    for j in range(1, A):
        aa = lax.rem(a + j, A)
        put(pred_tx.at[aa], pred_rx.at[aa], pr_ss.at[aa], pr_rs.at[aa], dev(aa, b, c)).wait_recv()
        total = total + pred_rx[aa].astype(jnp.float32)
    res = total.T - targ[...].astype(jnp.float32)
    resid[a] = res.astype(jnp.bfloat16)

    def res_copy(block, to):
        return put(resid.at[block], resid.at[block], re_ss.at[to], re_rs.at[block], dev(to, b, c))

    for j in range(1, A):
        res_copy(a, lax.rem(a + j, A)).start()
    res_out[...] = res
    for j in range(1, A):
        aa = lax.rem(a + j, A)
        res_copy(aa, aa).wait_recv()

    r = resid[...].reshape(A * R, resid.shape[2])

    def g_copy(cb, bb, cc):
        return put(g_tx.at[cb], g_rx.at[me_cb], g_ss.at[cb], g_rs.at[me_cb], dev(a, bb, cc))

    order = [(j, k) for j in range(1, B) for k in range(2)] + [(0, 1)]
    for j, k in order:
        bb, cc = lax.rem(b + j, B), lax.rem(c + k, 2)
        cb = bb * 2 + cc
        g_tx[cb] = jnp.dot(kt[cb], r, preferred_element_type=jnp.float32).astype(GRAD)
        g_copy(cb, bb, cc).start()
    g = jnp.dot(kt[me_cb], r, preferred_element_type=jnp.float32)
    for j, k in reversed(order):
        bb, cc = lax.rem(b + j, B), lax.rem(c + k, 2)
        cb = bb * 2 + cc
        put(g_tx.at[cb], g_rx.at[cb], g_ss.at[cb], g_rs.at[cb], dev(a, bb, cc)).wait_recv()
        g = g + g_rx[cb].astype(jnp.float32)
    g_own[...] = g

    n = inv.shape[1]
    for i in range(inv.shape[0]):
        at = pl.ds(i * n, n)
        cond = jnp.dot(
            inv[i], g_own[at, :], precision=lax.Precision.HIGHEST, preferred_element_type=jnp.float32
        )
        new = 0.9 * mom[at, :] + cond / batch
        mom_out[at, :] = new
        coef_out[at, :] = coef[at, :] - 0.5 * new

    @pl.when(a < A - 1)
    def _():
        row_copy(a, 0).wait_send()

    @pl.when(a > 0)
    def _():
        row_copy(a, 1).wait_send()

    def sent_rows(block, d):
        if d == 0:
            @pl.when(a < A - 1)
            def _():
                row_copy(block, 0).wait_send()
        else:
            @pl.when(a > 0)
            def _():
                row_copy(block, 1).wait_send()

    for dist in range(1, A):
        each_at(dist, sent_rows)
    for j in range(1, B):
        bb = lax.rem(b + j, B)
        for slot in (bb, B + bb):
            cen_copy(me_cb, slot, mate).wait_send()
            coef_copy(me_cb, slot, mate).wait_send()
    cen_copy(me_cb, B + b, mate).wait_send()
    coef_copy(me_cb, B + b, mate).wait_send()
    for j in range(1, A):
        aa = lax.rem(a + j, A)
        pred_copy(aa).wait_send()
        res_copy(a, aa).wait_send()
    for j, k in order:
        bb, cc = lax.rem(b + j, B), lax.rem(c + k, 2)
        g_copy(bb * 2 + cc, bb, cc).wait_send()


def shards(A, B, features, centres, targets, coefficients, momentum, block_inverse):
    R, D = features.shape
    C, K = coefficients.shape
    G = 2 * B
    dma = pltpu.SemaphoreType.DMA
    vmem = pl.BlockSpec(memory_space=pltpu.VMEM)
    flops = 2 * A * R * G * C * (D + 2 * K)
    return pl.pallas_call(
        functools.partial(kernel, A, B, float(A * B * 2 * R)),
        out_shape=(
            jax.ShapeDtypeStruct((R, K), jnp.float32),
            jax.ShapeDtypeStruct((C, K), jnp.float32),
            jax.ShapeDtypeStruct((C, K), jnp.float32),
        ),
        in_specs=[vmem] * 6,
        out_specs=(vmem,) * 3,
        scratch_shapes=[
            pltpu.VMEM((A, R, D), jnp.bfloat16),
            pltpu.VMEM((A, 8, R), jnp.float32),
            pltpu.VMEM((G, C, D), jnp.bfloat16),
            pltpu.VMEM((G, C, 128), jnp.float32),
            pltpu.VMEM((G, K, C), jnp.bfloat16),
            pltpu.VMEM((G, C, A * R), jnp.bfloat16),
            pltpu.VMEM((K, R), jnp.float32),
            pltpu.VMEM((A, K, R), PRED),
            pltpu.VMEM((A, K, R), PRED),
            pltpu.VMEM((A, R, K), jnp.bfloat16),
            pltpu.VMEM((C, K), jnp.float32),
            pltpu.VMEM((G, C, K), GRAD),
            pltpu.VMEM((G, C, K), GRAD),
            dma((A, 2)), dma((A,)),
            dma((G,)), dma((G,)), dma((G,)), dma((G,)),
            dma((A,)), dma((A,)), dma((A,)), dma((A,)),
            dma((G,)), dma((G,)),
        ],
        compiler_params=pltpu.CompilerParams(
            collective_id=0, has_side_effects=True, vmem_limit_bytes=40 * 1024 * 1024
        ),
        cost_estimate=pl.CostEstimate(
            flops=flops, bytes_accessed=4 * C * (C + 4 * K), transcendentals=A * R * G * C
        ),
    )(features, centres, targets, coefficients, momentum, block_inverse)


def solution(mesh):
    chips = mesh.shape["wide"] // 2
    B = 1 << ((chips.bit_length() - 1) // 2)
    A = chips // B
    two = P(("groups", "wide"), None)
    return jax.shard_map(
        functools.partial(shards, A, B),
        mesh=mesh,
        in_specs=(two, two, two, two, two, P(("groups", "wide"), None, None)),
        out_specs=(two, two, two),
        check_vma=False,
    )
```

```python
import functools
import itertools

import jax
import jax.numpy as jnp
from jax import lax
from jax.experimental import pallas as pl
from jax.experimental.pallas import tpu as pltpu
from jax.sharding import PartitionSpec as P

MESH = pl.DeviceIdType.MESH
PRED = jnp.bfloat16
GRAD = jnp.bfloat16
H = 2
Q = 4


def kernel(
    A, B,
    feat, cen, targ, coef, inv,
    res_out, cond_out,
    coef_own, targ_own, inv_own, in_sem,
    rows, rnorm, cens, cnorm, coefs, kt, own_pred, pred_tx, pred_rx, resid, g_own, g_tx, g_rx,
    row_ss, row_rs, cen_ss, cen_rs, cf_ss, cf_rs, pr_ss, pr_rs, re_ss, re_rs, g_ss, g_rs,
):
    w = lax.axis_index("wide")
    c = lax.rem(w, 2)
    chip = w // 2
    b = lax.rem(chip, B)
    a = chip // B
    R, C = feat.shape[0], cen.shape[0]
    scale = 2.0 / feat.shape[1]

    def dev(aa, bb, cc):
        return {"wide": (aa * B + bb) * 2 + cc}

    def put(src, dst, ss, rs, to):
        return pltpu.make_async_remote_copy(
            src_ref=src, dst_ref=dst, send_sem=ss, recv_sem=rs, device_id=to, device_id_type=MESH
        )

    me_cb = b * 2 + c
    mate_cb = b * 2 + (1 - c)
    mate = dev(a, b, 1 - c)

    barrier = pltpu.get_barrier_semaphore()
    for j in range(1, A):
        pl.semaphore_signal(barrier, inc=1, device_id=dev(lax.rem(a + j, A), b, c), device_id_type=MESH)
    for j in range(B):
        for k in range(2):
            if j or k:
                pl.semaphore_signal(
                    barrier, inc=1, device_id=dev(a, lax.rem(b + j, B), lax.rem(c + k, 2)), device_id_type=MESH
                )

    loads = [
        pltpu.make_async_copy(src, dst, in_sem.at[i])
        for i, (src, dst) in enumerate(
            [(feat, rows.at[a]), (cen, cens.at[me_cb]), (coef, coef_own), (targ, targ_own), (inv, inv_own)]
        )
    ]
    for load in loads:
        load.start()

    def row_copy(block, d, h):
        to = a + 1 if d == 0 else a - 1
        part = rows.at[block, pl.ds(h * (R // H), R // H)]
        return put(part, part, row_ss.at[block, d, h], row_rs.at[block, h], dev(to, b, c))

    def cen_copy(cb, slot, q, to):
        part = cens.at[cb, pl.ds(q * (C // Q), C // Q)]
        return put(part, part, cen_ss.at[slot, q], cen_rs.at[cb, q], to)

    def coef_copy(cb, slot, to):
        return put(coefs.at[cb], coefs.at[cb], cf_ss.at[slot], cf_rs.at[cb], to)

    loads[0].wait()
    loads[1].wait()
    pl.semaphore_wait(barrier, A - 1 + 2 * B - 1)

    @pl.when(a < A - 1)
    def _():
        for h in range(H):
            row_copy(a, 0, h).start()

    @pl.when(a > 0)
    def _():
        for h in range(H):
            row_copy(a, 1, h).start()

    for j in range(1, B):
        bb = lax.rem(b + j, B)
        for q in range(Q):
            cen_copy(me_cb, bb, q, dev(a, bb, c)).start()
    for q in range(Q):
        cen_copy(me_cb, B + b, q, mate).start()
    loads[2].wait()
    coefs[me_cb] = coef_own[...].astype(jnp.bfloat16).T
    for j in range(1, B):
        bb = lax.rem(b + j, B)
        coef_copy(me_cb, bb, dev(a, bb, c)).start()
    coef_copy(me_cb, B + b, mate).start()

    def row_norm(block):
        x = rows[block].astype(jnp.float32)
        s = jnp.sum(x * x, axis=1, keepdims=True)
        rnorm[block] = jnp.broadcast_to(s, (R, 128)).T[0:8]

    def cen_norm(cb):
        x = cens[cb].astype(jnp.float32)
        s = jnp.sum(x * x, axis=1, keepdims=True)
        cnorm[cb] = jnp.broadcast_to(s, (x.shape[0], 128))

    def tile(block, cb):
        p = lax.dot_general(
            cens[cb], rows[block], (((1,), (1,)), ((), ())), preferred_element_type=jnp.float32
        )
        e = (2.0 * p - rnorm[block, 0:1, :] - cnorm[cb, :, 0:1]) * scale
        kt[cb, :, pl.ds(pl.multiple_of(block * R, R), R)] = jnp.exp(e).astype(jnp.bfloat16)

    def tiles(block, lo, hi):
        def step(i, carry):
            tile(block, lax.rem(b + i // 2, B) * 2 + lax.rem(c + lax.rem(i, 2), 2))
            return carry

        lax.fori_loop(lo, hi, step, 0, unroll=2)

    def predict(block):
        def step(i, acc):
            k = kt[i, :, pl.ds(pl.multiple_of(block * R, R), R)]
            return acc + jnp.dot(coefs[i], k, preferred_element_type=jnp.float32)

        return lax.fori_loop(0, 2 * B, step, jnp.zeros((coefs.shape[1], R), jnp.float32), unroll=2)

    def pred_copy(block):
        return put(pred_tx.at[block], pred_rx.at[a], pr_ss.at[block], pr_rs.at[a], dev(block, b, c))

    def predict_and_send(block):
        pred_tx[block] = predict(block).astype(PRED)
        pred_copy(block).start()

    def each_at(dist, fn):
        @pl.when(a - dist >= 0)
        def _():
            fn(a - dist, 0)

        @pl.when(a + dist < A)
        def _():
            fn(a + dist, 1)

    def pass_rows(h, block, d):
        row_copy(block, d, h).wait_recv()
        if d == 0:
            @pl.when(a < A - 1)
            def _():
                row_copy(block, 0, h).start()
        else:
            @pl.when(a > 0)
            def _():
                row_copy(block, 1, h).start()

    def near(block, d):
        row_norm(block)
        tiles(block, 0, 2)

    def pass_centres(j, q):
        bb = lax.rem(b + j, B)
        cen_copy(bb * 2 + c, 0, q, mate).wait_recv()
        cen_copy(bb * 2 + c, B + bb, q, mate).start()

    row_norm(a)
    cen_norm(me_cb)
    tile(a, me_cb)
    for q in range(Q):
        cen_copy(mate_cb, 0, q, mate).wait_recv()
    cen_norm(mate_cb)
    tile(a, mate_cb)

    steps = itertools.zip_longest(
        [(dist, h) for dist in range(1, A - 1) for h in range(H)],
        [(j, q) for j in range(1, B) for q in range(Q)],
    )
    for row_step, cen_step in steps:
        if row_step is not None:
            dist, h = row_step
            each_at(dist, functools.partial(pass_rows, h))
        if cen_step is not None:
            pass_centres(*cen_step)
        if row_step is not None and h == H - 1:
            each_at(dist, near)

    for j in range(1, B):
        bb = lax.rem(b + j, B)
        coef_copy(bb * 2 + c, 0, mate).wait_recv()
        coef_copy(bb * 2 + c, B + bb, mate).start()
        cen_norm(bb * 2 + c)
    for j in range(1, B):
        bb = lax.rem(b + j, B)
        for q in range(Q):
            cen_copy(bb * 2 + 1 - c, 0, q, mate).wait_recv()
        cen_norm(bb * 2 + 1 - c)
    for dist in range(1, A - 1):
        each_at(dist, lambda block, d: tiles(block, 2, 2 * B))
    tiles(a, 2, 2 * B)

    coef_copy(mate_cb, 0, mate).wait_recv()
    for j in range(1, B):
        coef_copy(lax.rem(b + j, B) * 2 + 1 - c, 0, mate).wait_recv()
    for dist in range(A - 2, 0, -1):
        each_at(dist, lambda block, d: predict_and_send(block))

    def last(block, d):
        for h in range(H):
            pass_rows(h, block, d)
        row_norm(block)
        tiles(block, 0, 2 * B)
        predict_and_send(block)

    each_at(A - 1, last)
    own_pred[...] = predict(a)
    loads[3].wait()
    loads[4].wait()

    total = own_pred[...]
    for j in range(1, A):
        aa = lax.rem(a + j, A)
        put(pred_tx.at[aa], pred_rx.at[aa], pr_ss.at[aa], pr_rs.at[aa], dev(aa, b, c)).wait_recv()
        total = total + pred_rx[aa].astype(jnp.float32)
    res = total.T - targ_own[...].astype(jnp.float32)
    resid[a] = res.astype(jnp.bfloat16)

    def res_copy(block, to):
        return put(resid.at[block], resid.at[block], re_ss.at[to], re_rs.at[block], dev(to, b, c))

    for j in range(1, A):
        res_copy(a, lax.rem(a + j, A)).start()
    res_out[...] = res
    for j in range(1, A):
        aa = lax.rem(a + j, A)
        res_copy(aa, aa).wait_recv()

    r = resid[...].reshape(A * R, resid.shape[2])

    def g_copy(cb, bb, cc):
        return put(g_tx.at[cb], g_rx.at[me_cb], g_ss.at[cb], g_rs.at[me_cb], dev(a, bb, cc))

    order = [(j, k) for j in range(1, B) for k in range(2)] + [(0, 1)]
    for j, k in order:
        bb, cc = lax.rem(b + j, B), lax.rem(c + k, 2)
        cb = bb * 2 + cc
        g_tx[cb] = jnp.dot(kt[cb], r, preferred_element_type=jnp.float32).astype(GRAD)
        g_copy(cb, bb, cc).start()
    g = jnp.dot(kt[me_cb], r, preferred_element_type=jnp.float32)
    for j, k in reversed(order):
        bb, cc = lax.rem(b + j, B), lax.rem(c + k, 2)
        cb = bb * 2 + cc
        put(g_tx.at[cb], g_rx.at[cb], g_ss.at[cb], g_rs.at[cb], dev(a, bb, cc)).wait_recv()
        g = g + g_rx[cb].astype(jnp.float32)
    g_own[...] = g

    n = inv.shape[1]
    for i in range(inv.shape[0]):
        at = pl.ds(i * n, n)
        cond_out[at, :] = jnp.dot(
            inv_own[i], g_own[at, :], precision=lax.Precision.HIGHEST, preferred_element_type=jnp.float32
        )

    def sent_rows(block, d):
        if d == 0:
            @pl.when(a < A - 1)
            def _():
                for h in range(H):
                    row_copy(block, 0, h).wait_send()
        else:
            @pl.when(a > 0)
            def _():
                for h in range(H):
                    row_copy(block, 1, h).wait_send()

    sent_rows(a, 0)
    sent_rows(a, 1)
    for dist in range(1, A):
        each_at(dist, sent_rows)
    for j in range(1, B):
        bb = lax.rem(b + j, B)
        for slot in (bb, B + bb):
            for q in range(Q):
                cen_copy(me_cb, slot, q, mate).wait_send()
            coef_copy(me_cb, slot, mate).wait_send()
    for q in range(Q):
        cen_copy(me_cb, B + b, q, mate).wait_send()
    coef_copy(me_cb, B + b, mate).wait_send()
    for j in range(1, A):
        aa = lax.rem(a + j, A)
        pred_copy(aa).wait_send()
        res_copy(a, aa).wait_send()
    for j, k in order:
        bb, cc = lax.rem(b + j, B), lax.rem(c + k, 2)
        g_copy(bb * 2 + cc, bb, cc).wait_send()


def shards(A, B, features, centres, targets, coefficients, momentum, block_inverse):
    R, D = features.shape
    C, K = coefficients.shape
    G = 2 * B
    dma = pltpu.SemaphoreType.DMA
    vmem = pl.BlockSpec(memory_space=pltpu.VMEM)
    hbm = pl.BlockSpec(memory_space=pltpu.HBM)
    residual, conditioned = pl.pallas_call(
        functools.partial(kernel, A, B),
        out_shape=(jax.ShapeDtypeStruct((R, K), jnp.float32), jax.ShapeDtypeStruct((C, K), jnp.float32)),
        in_specs=[hbm] * 5,
        out_specs=(vmem,) * 2,
        scratch_shapes=[
            pltpu.VMEM((C, K), jnp.float32),
            pltpu.VMEM((R, K), jnp.bfloat16),
            pltpu.VMEM(block_inverse.shape, jnp.float32),
            dma((5,)),
            pltpu.VMEM((A, R, D), jnp.bfloat16),
            pltpu.VMEM((A, 8, R), jnp.float32),
            pltpu.VMEM((G, C, D), jnp.bfloat16),
            pltpu.VMEM((G, C, 128), jnp.float32),
            pltpu.VMEM((G, K, C), jnp.bfloat16),
            pltpu.VMEM((G, C, A * R), jnp.bfloat16),
            pltpu.VMEM((K, R), jnp.float32),
            pltpu.VMEM((A, K, R), PRED),
            pltpu.VMEM((A, K, R), PRED),
            pltpu.VMEM((A, R, K), jnp.bfloat16),
            pltpu.VMEM((C, K), jnp.float32),
            pltpu.VMEM((G, C, K), GRAD),
            pltpu.VMEM((G, C, K), GRAD),
            dma((A, 2, H)), dma((A, H)),
            dma((G, Q)), dma((G, Q)), dma((G,)), dma((G,)),
            dma((A,)), dma((A,)), dma((A,)), dma((A,)),
            dma((G,)), dma((G,)),
        ],
        compiler_params=pltpu.CompilerParams(
            collective_id=0, has_side_effects=True, vmem_limit_bytes=63 * 1024 * 1024
        ),
        cost_estimate=pl.CostEstimate(
            flops=2 * A * R * G * C * (D + 2 * K),
            bytes_accessed=4 * C * (C + 4 * K),
            transcendentals=A * R * G * C,
        ),
    )(features, centres, targets, coefficients, block_inverse)
    new_momentum = 0.9 * momentum + conditioned / (A * B * 2 * R)
    return residual, new_momentum, coefficients - 0.5 * new_momentum


def solution(mesh):
    chips = mesh.shape["wide"] // 2
    B = 1 << ((chips.bit_length() - 1) // 2)
    A = chips // B
    two = P(("groups", "wide"), None)
    return jax.shard_map(
        functools.partial(shards, A, B),
        mesh=mesh,
        in_specs=(two, two, two, two, two, P(("groups", "wide"), None, None)),
        out_specs=(two, two, two),
        check_vma=False,
    )
```

```python
import functools
import itertools

import jax
import jax.numpy as jnp
from jax import lax
from jax.experimental import pallas as pl
from jax.experimental.pallas import tpu as pltpu
from jax.sharding import PartitionSpec as P

MESH = pl.DeviceIdType.MESH
PRED = jnp.bfloat16
GRAD = jnp.bfloat16
H = 1
Q = 1


def kernel(
    A, B,
    feat, cen, targ, coef, inv,
    res_out, cond_out,
    coef_own, targ_own, inv_own, in_sem,
    rows, rnorm, cens, cnorm, coefs, kt, own_pred, pred_tx, pred_rx, resid, g_own, g_tx, g_rx,
    row_ss, row_rs, cen_ss, cen_rs, cf_ss, cf_rs, pr_ss, pr_rs, re_ss, re_rs, g_ss, g_rs,
):
    w = lax.axis_index("wide")
    c = lax.rem(w, 2)
    chip = w // 2
    b = lax.rem(chip, B)
    a = chip // B
    R, C = feat.shape[0], cen.shape[0]
    scale = 2.0 / feat.shape[1]

    def dev(aa, bb, cc):
        return {"wide": (aa * B + bb) * 2 + cc}

    def put(src, dst, ss, rs, to):
        return pltpu.make_async_remote_copy(
            src_ref=src, dst_ref=dst, send_sem=ss, recv_sem=rs, device_id=to, device_id_type=MESH
        )

    me_cb = b * 2 + c
    mate_cb = b * 2 + (1 - c)
    mate = dev(a, b, 1 - c)

    barrier = pltpu.get_barrier_semaphore()
    for j in range(1, A):
        pl.semaphore_signal(barrier, inc=1, device_id=dev(lax.rem(a + j, A), b, c), device_id_type=MESH)
    for j in range(B):
        for k in range(2):
            if j or k:
                pl.semaphore_signal(
                    barrier, inc=1, device_id=dev(a, lax.rem(b + j, B), lax.rem(c + k, 2)), device_id_type=MESH
                )

    loads = [
        pltpu.make_async_copy(src, dst, in_sem.at[i])
        for i, (src, dst) in enumerate(
            [(feat, rows.at[a]), (cen, cens.at[me_cb]), (coef, coef_own), (targ, targ_own), (inv, inv_own)]
        )
    ]
    for load in loads:
        load.start()

    def row_copy(block, d, step, h):
        to = a + step if d == 0 else a - step
        part = rows.at[block, pl.ds(h * (R // H), R // H)]
        return put(part, part, row_ss.at[block, d, step - 1, h], row_rs.at[block, h], dev(to, b, c))

    def onward(block, d, pieces, act):
        for step in (2, 1):
            @pl.when(a + step < A if d == 0 else a - step >= 0)
            def _():
                for h in pieces:
                    act(row_copy(block, d, step, h))

    start = lambda copy: copy.start()
    wait_send = lambda copy: copy.wait_send()

    def cen_copy(cb, slot, q, to):
        part = cens.at[cb, pl.ds(q * (C // Q), C // Q)]
        return put(part, part, cen_ss.at[slot, q], cen_rs.at[cb, q], to)

    def coef_copy(cb, slot, to):
        return put(coefs.at[cb], coefs.at[cb], cf_ss.at[slot], cf_rs.at[cb], to)

    loads[0].wait()
    loads[1].wait()
    pl.semaphore_wait(barrier, A - 1 + 2 * B - 1)

    onward(a, 0, range(H), start)
    onward(a, 1, range(H), start)

    for j in range(1, B):
        bb = lax.rem(b + j, B)
        for q in range(Q):
            cen_copy(me_cb, bb, q, dev(a, bb, c)).start()
    for q in range(Q):
        cen_copy(me_cb, B + b, q, mate).start()
    loads[2].wait()
    coefs[me_cb] = coef_own[...].astype(jnp.bfloat16).T
    for j in range(1, B):
        bb = lax.rem(b + j, B)
        coef_copy(me_cb, bb, dev(a, bb, c)).start()
    coef_copy(me_cb, B + b, mate).start()

    def row_norm(block):
        x = rows[block].astype(jnp.float32)
        s = jnp.sum(x * x, axis=1, keepdims=True)
        rnorm[block] = jnp.broadcast_to(s, (R, 128)).T[0:8]

    def cen_norm(cb):
        x = cens[cb].astype(jnp.float32)
        s = jnp.sum(x * x, axis=1, keepdims=True)
        cnorm[cb] = jnp.broadcast_to(s, (x.shape[0], 128))

    def tile(block, cb):
        p = lax.dot_general(
            cens[cb], rows[block], (((1,), (1,)), ((), ())), preferred_element_type=jnp.float32
        )
        e = (2.0 * p - rnorm[block, 0:1, :] - cnorm[cb, :, 0:1]) * scale
        kt[cb, :, pl.ds(pl.multiple_of(block * R, R), R)] = jnp.exp(e).astype(jnp.bfloat16)

    def tiles(block, lo, hi):
        def step(i, carry):
            tile(block, lax.rem(b + i // 2, B) * 2 + lax.rem(c + lax.rem(i, 2), 2))
            return carry

        lax.fori_loop(lo, hi, step, 0, unroll=2)

    def predict(block):
        def step(i, acc):
            k = kt[i, :, pl.ds(pl.multiple_of(block * R, R), R)]
            return acc + jnp.dot(coefs[i], k, preferred_element_type=jnp.float32)

        return lax.fori_loop(0, 2 * B, step, jnp.zeros((coefs.shape[1], R), jnp.float32), unroll=2)

    def pred_copy(block):
        return put(pred_tx.at[block], pred_rx.at[a], pr_ss.at[block], pr_rs.at[a], dev(block, b, c))

    def predict_and_send(block):
        pred_tx[block] = predict(block).astype(PRED)
        pred_copy(block).start()

    def each_at(dist, fn):
        @pl.when(a - dist >= 0)
        def _():
            fn(a - dist, 0)

        @pl.when(a + dist < A)
        def _():
            fn(a + dist, 1)

    def pass_rows(h, dist, block, d):
        row_copy(block, d, 1, h).wait_recv()
        if dist % 2 == 0:
            onward(block, d, [h], start)

    def near(block, d):
        row_norm(block)
        tiles(block, 0, 2)

    def pass_centres(j, q):
        bb = lax.rem(b + j, B)
        cen_copy(bb * 2 + c, 0, q, mate).wait_recv()
        cen_copy(bb * 2 + c, B + bb, q, mate).start()

    row_norm(a)
    cen_norm(me_cb)
    tile(a, me_cb)
    for q in range(Q):
        cen_copy(mate_cb, 0, q, mate).wait_recv()
    cen_norm(mate_cb)
    tile(a, mate_cb)

    steps = itertools.zip_longest(
        [(dist, h) for dist in range(2, A - 1) for h in range(H)],
        [(j, q) for j in range(1, B) for q in range(Q)],
    )
    for row_step, cen_step in steps:
        if row_step is not None:
            dist, h = row_step
            each_at(dist, functools.partial(pass_rows, h, dist))
        if cen_step is not None:
            pass_centres(*cen_step)

    for j in range(1, B):
        bb = lax.rem(b + j, B)
        coef_copy(bb * 2 + c, 0, mate).wait_recv()
        coef_copy(bb * 2 + c, B + bb, mate).start()
        cen_norm(bb * 2 + c)
    for h in range(H):
        each_at(1, functools.partial(pass_rows, h, 1))
    for dist in range(1, A - 1):
        each_at(dist, near)
    for j in range(1, B):
        bb = lax.rem(b + j, B)
        for q in range(Q):
            cen_copy(bb * 2 + 1 - c, 0, q, mate).wait_recv()
        cen_norm(bb * 2 + 1 - c)
    for dist in range(1, A - 1):
        each_at(dist, lambda block, d: tiles(block, 2, 2 * B))
    tiles(a, 2, 2 * B)

    coef_copy(mate_cb, 0, mate).wait_recv()
    for j in range(1, B):
        coef_copy(lax.rem(b + j, B) * 2 + 1 - c, 0, mate).wait_recv()
    for dist in range(A - 2, 0, -1):
        each_at(dist, lambda block, d: predict_and_send(block))

    def last(block, d):
        for h in range(H):
            pass_rows(h, A - 1, block, d)
        row_norm(block)
        tiles(block, 0, 2 * B)
        predict_and_send(block)

    each_at(A - 1, last)
    own_pred[...] = predict(a)
    loads[3].wait()
    loads[4].wait()

    total = own_pred[...]
    for j in range(1, A):
        aa = lax.rem(a + j, A)
        put(pred_tx.at[aa], pred_rx.at[aa], pr_ss.at[aa], pr_rs.at[aa], dev(aa, b, c)).wait_recv()
        total = total + pred_rx[aa].astype(jnp.float32)
    res = total.T - targ_own[...].astype(jnp.float32)
    resid[a] = res.astype(jnp.bfloat16)

    def res_copy(block, to):
        return put(resid.at[block], resid.at[block], re_ss.at[to], re_rs.at[block], dev(to, b, c))

    for j in range(1, A):
        res_copy(a, lax.rem(a + j, A)).start()
    res_out[...] = res
    for j in range(1, A):
        aa = lax.rem(a + j, A)
        res_copy(aa, aa).wait_recv()

    r = resid[...].reshape(A * R, resid.shape[2])

    def g_copy(cb, bb, cc):
        return put(g_tx.at[cb], g_rx.at[me_cb], g_ss.at[cb], g_rs.at[me_cb], dev(a, bb, cc))

    order = [(j, k) for j in range(1, B) for k in range(2)] + [(0, 1)]
    for j, k in order:
        bb, cc = lax.rem(b + j, B), lax.rem(c + k, 2)
        cb = bb * 2 + cc
        g_tx[cb] = jnp.dot(kt[cb], r, preferred_element_type=jnp.float32).astype(GRAD)
        g_copy(cb, bb, cc).start()
    g = jnp.dot(kt[me_cb], r, preferred_element_type=jnp.float32)
    for j, k in reversed(order):
        bb, cc = lax.rem(b + j, B), lax.rem(c + k, 2)
        cb = bb * 2 + cc
        put(g_tx.at[cb], g_rx.at[cb], g_ss.at[cb], g_rs.at[cb], dev(a, bb, cc)).wait_recv()
        g = g + g_rx[cb].astype(jnp.float32)
    g_own[...] = g

    n = inv.shape[1]
    for i in range(inv.shape[0]):
        at = pl.ds(i * n, n)
        cond_out[at, :] = jnp.dot(
            inv_own[i], g_own[at, :], precision=lax.Precision.HIGHEST, preferred_element_type=jnp.float32
        )

    onward(a, 0, range(H), wait_send)
    onward(a, 1, range(H), wait_send)
    for dist in range(2, A, 2):
        each_at(dist, lambda block, d: onward(block, d, range(H), wait_send))
    for j in range(1, B):
        bb = lax.rem(b + j, B)
        for slot in (bb, B + bb):
            for q in range(Q):
                cen_copy(me_cb, slot, q, mate).wait_send()
            coef_copy(me_cb, slot, mate).wait_send()
    for q in range(Q):
        cen_copy(me_cb, B + b, q, mate).wait_send()
    coef_copy(me_cb, B + b, mate).wait_send()
    for j in range(1, A):
        aa = lax.rem(a + j, A)
        pred_copy(aa).wait_send()
        res_copy(a, aa).wait_send()
    for j, k in order:
        bb, cc = lax.rem(b + j, B), lax.rem(c + k, 2)
        g_copy(bb * 2 + cc, bb, cc).wait_send()


def shards(A, B, features, centres, targets, coefficients, momentum, block_inverse):
    R, D = features.shape
    C, K = coefficients.shape
    G = 2 * B
    dma = pltpu.SemaphoreType.DMA
    vmem = pl.BlockSpec(memory_space=pltpu.VMEM)
    hbm = pl.BlockSpec(memory_space=pltpu.HBM)
    residual, conditioned = pl.pallas_call(
        functools.partial(kernel, A, B),
        out_shape=(jax.ShapeDtypeStruct((R, K), jnp.float32), jax.ShapeDtypeStruct((C, K), jnp.float32)),
        in_specs=[hbm] * 5,
        out_specs=(vmem,) * 2,
        scratch_shapes=[
            pltpu.VMEM((C, K), jnp.float32),
            pltpu.VMEM((R, K), jnp.bfloat16),
            pltpu.VMEM(block_inverse.shape, jnp.float32),
            dma((5,)),
            pltpu.VMEM((A, R, D), jnp.bfloat16),
            pltpu.VMEM((A, 8, R), jnp.float32),
            pltpu.VMEM((G, C, D), jnp.bfloat16),
            pltpu.VMEM((G, C, 128), jnp.float32),
            pltpu.VMEM((G, K, C), jnp.bfloat16),
            pltpu.VMEM((G, C, A * R), jnp.bfloat16),
            pltpu.VMEM((K, R), jnp.float32),
            pltpu.VMEM((A, K, R), PRED),
            pltpu.VMEM((A, K, R), PRED),
            pltpu.VMEM((A, R, K), jnp.bfloat16),
            pltpu.VMEM((C, K), jnp.float32),
            pltpu.VMEM((G, C, K), GRAD),
            pltpu.VMEM((G, C, K), GRAD),
            dma((A, 2, 2, H)), dma((A, H)),
            dma((G, Q)), dma((G, Q)), dma((G,)), dma((G,)),
            dma((A,)), dma((A,)), dma((A,)), dma((A,)),
            dma((G,)), dma((G,)),
        ],
        compiler_params=pltpu.CompilerParams(
            collective_id=0, has_side_effects=True, vmem_limit_bytes=63 * 1024 * 1024
        ),
        cost_estimate=pl.CostEstimate(
            flops=2 * A * R * G * C * (D + 2 * K),
            bytes_accessed=4 * C * (C + 4 * K),
            transcendentals=A * R * G * C,
        ),
    )(features, centres, targets, coefficients, block_inverse)
    return pl.pallas_call(
        functools.partial(update, float(A * B * 2 * R)),
        out_shape=(
            jax.ShapeDtypeStruct((R, K), jnp.float32),
            jax.ShapeDtypeStruct((C, K), jnp.float32),
            jax.ShapeDtypeStruct((C, K), jnp.float32),
        ),
        in_specs=[vmem] * 4,
        out_specs=(vmem,) * 3,

    )(residual, conditioned, momentum, coefficients)


def update(batch, res, cond, mom, coef, res_out, mom_out, coef_out):
    res_out[...] = res[...]
    new = 0.9 * mom[...] + cond[...] / batch
    mom_out[...] = new
    coef_out[...] = coef[...] - 0.5 * new


def solution(mesh):
    chips = mesh.shape["wide"] // 2
    B = 1 << ((chips.bit_length() - 1) // 2)
    A = chips // B
    two = P(("groups", "wide"), None)
    return jax.shard_map(
        functools.partial(shards, A, B),
        mesh=mesh,
        in_specs=(two, two, two, two, two, P(("groups", "wide"), None, None)),
        out_specs=(two, two, two),
        check_vma=False,
    )
```

```python
import functools
import itertools

import jax
import jax.numpy as jnp
from jax import lax
from jax.experimental import pallas as pl
from jax.experimental.pallas import tpu as pltpu
from jax.sharding import PartitionSpec as P

MESH = pl.DeviceIdType.MESH
PRED = jnp.bfloat16
GRAD = jnp.bfloat16
H = 1
Q = 1


def kernel(
    A, B,
    feat, cen, targ, coef, inv,
    res_out, cond_out,
    coef_own, targ_own, inv_own, in_sem,
    rows, rnorm, cens, cnorm, coefs, kt, own_pred, pred_tx, pred_rx, resid, g_own, g_tx, g_rx,
    row_ss, row_rs, cen_ss, cen_rs, cf_ss, cf_rs, pr_ss, pr_rs, re_ss, re_rs, g_ss, g_rs,
):
    w = lax.axis_index("wide")
    c = lax.rem(w, 2)
    chip = w // 2
    b = lax.rem(chip, B)
    a = chip // B
    R, C = feat.shape[0], cen.shape[0]
    scale = 2.0 / feat.shape[1]

    def dev(aa, bb, cc):
        return {"wide": (aa * B + bb) * 2 + cc}

    def put(src, dst, ss, rs, to):
        return pltpu.make_async_remote_copy(
            src_ref=src, dst_ref=dst, send_sem=ss, recv_sem=rs, device_id=to, device_id_type=MESH
        )

    me_cb = b * 2 + c
    mate_cb = b * 2 + (1 - c)
    mate = dev(a, b, 1 - c)

    barrier = pltpu.get_barrier_semaphore()
    for j in range(1, A):
        pl.semaphore_signal(barrier, inc=1, device_id=dev(lax.rem(a + j, A), b, c), device_id_type=MESH)
    for j in range(B):
        for k in range(2):
            if j or k:
                pl.semaphore_signal(
                    barrier, inc=1, device_id=dev(a, lax.rem(b + j, B), lax.rem(c + k, 2)), device_id_type=MESH
                )

    loads = [
        pltpu.make_async_copy(src, dst, in_sem.at[i])
        for i, (src, dst) in enumerate(
            [(feat, rows.at[a]), (cen, cens.at[me_cb]), (coef, coef_own), (targ, targ_own), (inv, inv_own)]
        )
    ]
    for load in loads:
        load.start()

    def row_copy(block, d, step, h):
        to = a + step if d == 0 else a - step
        part = rows.at[block, pl.ds(h * (R // H), R // H)]
        return put(part, part, row_ss.at[block, d, step - 1, h], row_rs.at[block, h], dev(to, b, c))

    def onward(block, d, pieces, act):
        for step in (2, 1):
            @pl.when(a + step < A if d == 0 else a - step >= 0)
            def _():
                for h in pieces:
                    act(row_copy(block, d, step, h))

    start = lambda copy: copy.start()
    wait_send = lambda copy: copy.wait_send()

    def cen_copy(cb, slot, q, to):
        part = cens.at[cb, pl.ds(q * (C // Q), C // Q)]
        return put(part, part, cen_ss.at[slot, q], cen_rs.at[cb, q], to)

    def coef_copy(cb, slot, to):
        return put(coefs.at[cb], coefs.at[cb], cf_ss.at[slot], cf_rs.at[cb], to)

    loads[0].wait()
    loads[1].wait()
    pl.semaphore_wait(barrier, A - 1 + 2 * B - 1)

    onward(a, 0, range(H), start)
    onward(a, 1, range(H), start)

    for j in range(1, B):
        bb = lax.rem(b + j, B)
        for q in range(Q):
            cen_copy(me_cb, bb, q, dev(a, bb, c)).start()
    for q in range(Q):
        cen_copy(me_cb, B + b, q, mate).start()
    loads[2].wait()
    coefs[me_cb] = coef_own[...].astype(jnp.bfloat16).T
    for j in range(1, B):
        bb = lax.rem(b + j, B)
        coef_copy(me_cb, bb, dev(a, bb, c)).start()
    coef_copy(me_cb, B + b, mate).start()

    def row_norm(block):
        x = rows[block].astype(jnp.float32)
        s = jnp.sum(x * x, axis=1, keepdims=True)
        rnorm[block] = jnp.broadcast_to(s, (R, 128)).T[0:8]

    def cen_norm(cb):
        x = cens[cb].astype(jnp.float32)
        s = jnp.sum(x * x, axis=1, keepdims=True)
        cnorm[cb] = jnp.broadcast_to(s, (x.shape[0], 128))

    def tile(block, cb):
        p = lax.dot_general(
            cens[cb], rows[block], (((1,), (1,)), ((), ())), preferred_element_type=jnp.float32
        )
        e = (2.0 * p - rnorm[block, 0:1, :] - cnorm[cb, :, 0:1]) * scale
        kt[cb, :, pl.ds(pl.multiple_of(block * R, R), R)] = jnp.exp(e).astype(jnp.bfloat16)

    def tiles(block, lo, hi):
        def step(i, carry):
            tile(block, lax.rem(b + i // 2, B) * 2 + lax.rem(c + lax.rem(i, 2), 2))
            return carry

        lax.fori_loop(lo, hi, step, 0, unroll=hi - lo)

    def predict(block):
        def step(i, acc):
            k = kt[i, :, pl.ds(pl.multiple_of(block * R, R), R)]
            return acc + jnp.dot(coefs[i], k, preferred_element_type=jnp.float32)

        return lax.fori_loop(0, 2 * B, step, jnp.zeros((coefs.shape[1], R), jnp.float32), unroll=4)

    def pred_copy(block):
        return put(pred_tx.at[block], pred_rx.at[a], pr_ss.at[block], pr_rs.at[a], dev(block, b, c))

    def predict_and_send(block):
        pred_tx[block] = predict(block).astype(PRED)
        pred_copy(block).start()

    def each_at(dist, fn):
        @pl.when(a - dist >= 0)
        def _():
            fn(a - dist, 0)

        @pl.when(a + dist < A)
        def _():
            fn(a + dist, 1)

    def pass_rows(h, dist, block, d):
        row_copy(block, d, 1, h).wait_recv()
        if dist % 2 == 0:
            onward(block, d, [h], start)

    def near(block, d):
        row_norm(block)
        tiles(block, 0, 2)

    def pass_centres(j, q):
        bb = lax.rem(b + j, B)
        cen_copy(bb * 2 + c, 0, q, mate).wait_recv()
        cen_copy(bb * 2 + c, B + bb, q, mate).start()

    row_norm(a)
    cen_norm(me_cb)
    tile(a, me_cb)
    steps = itertools.zip_longest(
        [(dist, h) for dist in range(2, A - 1) for h in range(H)],
        [(j, q) for j in range(1, B) for q in range(Q)],
    )
    for row_step, cen_step in steps:
        if row_step is not None:
            dist, h = row_step
            each_at(dist, functools.partial(pass_rows, h, dist))
        if cen_step is not None:
            pass_centres(*cen_step)

    for j in range(1, B):
        bb = lax.rem(b + j, B)
        coef_copy(bb * 2 + c, 0, mate).wait_recv()
        coef_copy(bb * 2 + c, B + bb, mate).start()
        cen_norm(bb * 2 + c)
    for q in range(Q):
        cen_copy(mate_cb, 0, q, mate).wait_recv()
    cen_norm(mate_cb)
    tile(a, mate_cb)

    for h in range(H):
        each_at(1, functools.partial(pass_rows, h, 1))
    for dist in range(1, A - 1):
        each_at(dist, near)
    for j in range(1, B):
        bb = lax.rem(b + j, B)
        for q in range(Q):
            cen_copy(bb * 2 + 1 - c, 0, q, mate).wait_recv()
        cen_norm(bb * 2 + 1 - c)
    for dist in range(1, A - 1):
        each_at(dist, lambda block, d: tiles(block, 2, 2 * B))
    tiles(a, 2, 2 * B)

    coef_copy(mate_cb, 0, mate).wait_recv()
    for j in range(1, B):
        coef_copy(lax.rem(b + j, B) * 2 + 1 - c, 0, mate).wait_recv()
    for dist in range(A - 2, 0, -1):
        each_at(dist, lambda block, d: predict_and_send(block))

    def last(block, d):
        for h in range(H):
            pass_rows(h, A - 1, block, d)
        row_norm(block)
        tiles(block, 0, 2 * B)
        predict_and_send(block)

    each_at(A - 1, last)
    own_pred[...] = predict(a)
    loads[3].wait()
    loads[4].wait()

    total = own_pred[...]
    for j in range(1, A):
        aa = lax.rem(a + j, A)
        put(pred_tx.at[aa], pred_rx.at[aa], pr_ss.at[aa], pr_rs.at[aa], dev(aa, b, c)).wait_recv()
        total = total + pred_rx[aa].astype(jnp.float32)
    res = total.T - targ_own[...].astype(jnp.float32)
    resid[a] = res.astype(jnp.bfloat16)

    def res_copy(block, to):
        return put(resid.at[block], resid.at[block], re_ss.at[to], re_rs.at[block], dev(to, b, c))

    for j in range(1, A):
        res_copy(a, lax.rem(a + j, A)).start()
    res_out[...] = res
    for j in range(1, A):
        aa = lax.rem(a + j, A)
        res_copy(aa, aa).wait_recv()

    r = resid[...].reshape(A * R, resid.shape[2])

    def g_copy(cb, bb, cc):
        return put(g_tx.at[cb], g_rx.at[me_cb], g_ss.at[cb], g_rs.at[me_cb], dev(a, bb, cc))

    order = [(j, k) for j in range(1, B) for k in range(2)] + [(0, 1)]
    for j, k in order:
        bb, cc = lax.rem(b + j, B), lax.rem(c + k, 2)
        cb = bb * 2 + cc
        g_tx[cb] = jnp.dot(kt[cb], r, preferred_element_type=jnp.float32).astype(GRAD)
        g_copy(cb, bb, cc).start()
    g = jnp.dot(kt[me_cb], r, preferred_element_type=jnp.float32)
    for j, k in reversed(order):
        bb, cc = lax.rem(b + j, B), lax.rem(c + k, 2)
        cb = bb * 2 + cc
        put(g_tx.at[cb], g_rx.at[cb], g_ss.at[cb], g_rs.at[cb], dev(a, bb, cc)).wait_recv()
        g = g + g_rx[cb].astype(jnp.float32)
    g_own[...] = g

    n = inv.shape[1]
    for i in range(inv.shape[0]):
        at = pl.ds(i * n, n)
        cond_out[at, :] = jnp.dot(
            inv_own[i], g_own[at, :], precision=lax.Precision.HIGHEST, preferred_element_type=jnp.float32
        )

    onward(a, 0, range(H), wait_send)
    onward(a, 1, range(H), wait_send)
    for dist in range(2, A, 2):
        each_at(dist, lambda block, d: onward(block, d, range(H), wait_send))
    for j in range(1, B):
        bb = lax.rem(b + j, B)
        for slot in (bb, B + bb):
            for q in range(Q):
                cen_copy(me_cb, slot, q, mate).wait_send()
            coef_copy(me_cb, slot, mate).wait_send()
    for q in range(Q):
        cen_copy(me_cb, B + b, q, mate).wait_send()
    coef_copy(me_cb, B + b, mate).wait_send()
    for j in range(1, A):
        aa = lax.rem(a + j, A)
        pred_copy(aa).wait_send()
        res_copy(a, aa).wait_send()
    for j, k in order:
        bb, cc = lax.rem(b + j, B), lax.rem(c + k, 2)
        g_copy(bb * 2 + cc, bb, cc).wait_send()


def shards(A, B, features, centres, targets, coefficients, momentum, block_inverse):
    R, D = features.shape
    C, K = coefficients.shape
    G = 2 * B
    dma = pltpu.SemaphoreType.DMA
    vmem = pl.BlockSpec(memory_space=pltpu.VMEM)
    hbm = pl.BlockSpec(memory_space=pltpu.HBM)
    residual, conditioned = pl.pallas_call(
        functools.partial(kernel, A, B),
        out_shape=(jax.ShapeDtypeStruct((R, K), jnp.float32), jax.ShapeDtypeStruct((C, K), jnp.float32)),
        in_specs=[hbm] * 5,
        out_specs=(vmem,) * 2,
        scratch_shapes=[
            pltpu.VMEM((C, K), jnp.float32),
            pltpu.VMEM((R, K), jnp.bfloat16),
            pltpu.VMEM(block_inverse.shape, jnp.float32),
            dma((5,)),
            pltpu.VMEM((A, R, D), jnp.bfloat16),
            pltpu.VMEM((A, 8, R), jnp.float32),
            pltpu.VMEM((G, C, D), jnp.bfloat16),
            pltpu.VMEM((G, C, 128), jnp.float32),
            pltpu.VMEM((G, K, C), jnp.bfloat16),
            pltpu.VMEM((G, C, A * R), jnp.bfloat16),
            pltpu.VMEM((K, R), jnp.float32),
            pltpu.VMEM((A, K, R), PRED),
            pltpu.VMEM((A, K, R), PRED),
            pltpu.VMEM((A, R, K), jnp.bfloat16),
            pltpu.VMEM((C, K), jnp.float32),
            pltpu.VMEM((G, C, K), GRAD),
            pltpu.VMEM((G, C, K), GRAD),
            dma((A, 2, 2, H)), dma((A, H)),
            dma((G, Q)), dma((G, Q)), dma((G,)), dma((G,)),
            dma((A,)), dma((A,)), dma((A,)), dma((A,)),
            dma((G,)), dma((G,)),
        ],
        compiler_params=pltpu.CompilerParams(
            collective_id=0, has_side_effects=True, vmem_limit_bytes=63 * 1024 * 1024
        ),
        cost_estimate=pl.CostEstimate(
            flops=2 * A * R * G * C * (D + 2 * K),
            bytes_accessed=4 * C * (C + 4 * K),
            transcendentals=A * R * G * C,
        ),
    )(features, centres, targets, coefficients, block_inverse)
    return pl.pallas_call(
        functools.partial(update, float(A * B * 2 * R)),
        out_shape=(
            jax.ShapeDtypeStruct((R, K), jnp.float32),
            jax.ShapeDtypeStruct((C, K), jnp.float32),
            jax.ShapeDtypeStruct((C, K), jnp.float32),
        ),
        in_specs=[vmem] * 4,
        out_specs=(vmem,) * 3,

    )(residual, conditioned, momentum, coefficients)


def update(batch, res, cond, mom, coef, res_out, mom_out, coef_out):
    res_out[...] = res[...]
    new = 0.9 * mom[...] + cond[...] / batch
    mom_out[...] = new
    coef_out[...] = coef[...] - 0.5 * new


def solution(mesh):
    chips = mesh.shape["wide"] // 2
    B = 1 << ((chips.bit_length() - 1) // 2)
    A = chips // B
    two = P(("groups", "wide"), None)
    return jax.shard_map(
        functools.partial(shards, A, B),
        mesh=mesh,
        in_specs=(two, two, two, two, two, P(("groups", "wide"), None, None)),
        out_specs=(two, two, two),
        check_vma=False,
    )
```
